32 devices in a mesh: sec: 4 (over y, core), op: 8 (over z, x).
Axes of the slice: x: 2, y: 2, z: 4, core: 2. Of those that a mesh axis runs over, the one named last changes fastest.
Arguments:
- wavefunction: bfloat16 [8, 256, 256], P('sec'), may hold values from -6 to 6
- diagonal: bfloat16 [8, 256, 256], P('sec'), may hold values from 1 to 4
- preconditioner: bfloat16 [8, 256, 256], P('sec'), may hold values from 0.25 to 1
- left_operator_blocks: bfloat16 [512, 256, 256], P(('sec', 'op')), may hold values from -0.1875 to 0.1875
- right_operator_blocks: bfloat16 [512, 256, 256], P(('sec', 'op')), may hold values from -0.375 to 0.375
- slot_source_sector: int32 [512], P(('sec', 'op')), may hold values from 0 to 7
- slot_target_sector: int32 [512], P(('sec', 'op')), may hold values from 0 to 1
- pair_count: int32 [32], P(('sec', 'op')), may hold values from 1 to 16, as said below
- left_dims: int32 [8], replicated, may hold values from 128 to 256, as said below
- right_dims: int32 [8], replicated, may hold values from 128 to 256, as said below
Outputs:
- correction: bfloat16 [8, 256, 256], P('sec')
- product_rows: float32 [8, 256, 256], P('sec', 'op')
- projected: float32 [3], replicated
The draws below stay inside these ranges and needn't reach their ends.
Inputs may be any that keep to these rules, and one draw needn't show every extreme that they name: `pair_count`: slots below a device's count hold pairs, the rest are ignored; some device has all 16 slots live. `left_dims`: some sector uses all 256 rows. `right_dims`: some sector uses all 256 columns.
All inputs are finite; a program needn't handle non-finite values.
Results may differ from the reference program's by a relative error of at most 0.003.
Values may be sent and summed in bfloat16 or wider, within the bound.
A program may use at most 64 MiB of HBM per device.

```python
import math
import jax
import jax.numpy as jnp
from jax import lax

BLOCK_EXTENT = 256
DEVICE_SECTORS = 2
DEVICE_SLOTS = 16
SECTORS_TOTAL = 8
PAIR_SLOTS_TOTAL = 512
N_SEC = 4
N_OP = 8


def draw_pair_count(key, part):
    first_key, second_key, third_key = jax.random.split(jax.random.fold_in(key, 11), 3)
    device_count = N_SEC * N_OP
    smaller = jnp.minimum(jax.random.randint(first_key, (device_count,), 1, DEVICE_SLOTS + 1), jax.random.randint(second_key, (device_count,), 1, DEVICE_SLOTS + 1))
    chosen = jax.random.randint(third_key, (), 0, device_count)
    return jnp.where(jnp.arange(device_count) == chosen, DEVICE_SLOTS, smaller).astype(jnp.int32)


def draw_dims(key, salt_value):
    first_key, second_key = jax.random.split(jax.random.fold_in(key, salt_value))
    sizes_drawn = jax.random.randint(first_key, (SECTORS_TOTAL,), BLOCK_EXTENT // 2, BLOCK_EXTENT + 1)
    chosen = jax.random.randint(second_key, (), 0, SECTORS_TOTAL)
    return jnp.where(jnp.arange(SECTORS_TOTAL) == chosen, BLOCK_EXTENT, sizes_drawn).astype(jnp.int32)


def draw_left_dims(key, part):
    return draw_dims(key, 21)


def draw_right_dims(key, part):
    return draw_dims(key, 22)


def place_ends(values, rng, low, largest):
    longest = values.shape.index(max(values.shape))
    spots = []
    for shift in (0, 1):
        where = [jax.random.randint(jax.random.fold_in(rng, axis), (), 0, length) for axis, length in enumerate(values.shape)]
        where[longest] = (where[longest] + shift) % values.shape[longest]
        spots.append(tuple(where))
    return values.at[spots[0]].set(low).at[spots[1]].set(largest)


def with_spikes(array, stream_key, source, target, parts, factor):
    owner, partner = [(jnp.arange(array.shape[dim]) // (array.shape[dim] // parts)).reshape([-1 if axis == dim else 1 for axis in range(array.ndim)]) for dim in (source, target)]
    chosen = jax.random.permutation(stream_key, parts)[partner]
    strong = (owner == chosen) | (owner == (partner + parts // 2) % parts)
    return jnp.where(strong, factor * array, array)


def block_scale(own_key, shape, shards, smallest, largest):
    factor_of = 1.0
    for position, shards_of in shards:
        draws = jax.random.uniform(jax.random.fold_in(jax.random.fold_in(own_key, 6), position), (shards_of,), jnp.float32, smallest / len(shards), largest / len(shards))
        factor_of = factor_of * jnp.repeat(jnp.exp(draws), shape[position] // shards_of).reshape((-1,) + (1,) * (len(shape) - 1 - position))
    return factor_of


def scatter_about(stream_key, shape, deviation, reach, shards=(), kind=jnp.bfloat16):
    gain = block_scale(stream_key, shape, shards, -0.22, 0.18) if shards else 1.0
    values = jax.random.normal(stream_key, shape, jnp.float32) * deviation * gain
    return jnp.minimum(jnp.maximum(values, -reach), reach).astype(kind)


def noise_with(stream_key, extent, width, reach, cuts, heavy, kind=jnp.bfloat16):
    values = width * jax.random.normal(stream_key, extent, jnp.float32)
    if cuts:
        values = values * block_scale(stream_key, extent, cuts, -0.22, 0.18)
    return jnp.clip(with_spikes(values, jax.random.fold_in(stream_key, 3), *heavy), -reach, reach).astype(kind)


def setup_inputs(seed: int = 0) -> dict:
    key_of = jax.random.split(jax.random.key(seed), 11)
    return {
        "wavefunction": scatter_about(key_of[0], (SECTORS_TOTAL, BLOCK_EXTENT, BLOCK_EXTENT), 1.0, 6.0, ((0, 4),)),
        "diagonal": jnp.clip(jnp.exp(math.log(4.0) - 1.3862944 * jax.random.uniform(key_of[1], (SECTORS_TOTAL, BLOCK_EXTENT, BLOCK_EXTENT), jnp.float32) ** block_scale(key_of[1], (SECTORS_TOTAL, BLOCK_EXTENT, BLOCK_EXTENT), ((0, 4),), -0.2, 0.2)), 1.0, 4.0).astype(jnp.bfloat16),
        "preconditioner": jnp.clip(jnp.exp(math.log(1.0) - 1.3862944 * jax.random.uniform(key_of[2], (SECTORS_TOTAL, BLOCK_EXTENT, BLOCK_EXTENT), jnp.float32) ** block_scale(key_of[2], (SECTORS_TOTAL, BLOCK_EXTENT, BLOCK_EXTENT), ((0, 4),), -0.2, 0.2)), 0.25, 1.0).astype(jnp.bfloat16),
        "left_operator_blocks": noise_with(key_of[3], (PAIR_SLOTS_TOTAL, BLOCK_EXTENT, BLOCK_EXTENT), (BLOCK_EXTENT * DEVICE_SLOTS * N_OP // (4 * DEVICE_SECTORS)) ** -0.5, 0.1875, ((0, 32),), (0, 1, 32, 2.75)),
        "right_operator_blocks": scatter_about(key_of[4], (PAIR_SLOTS_TOTAL, BLOCK_EXTENT, BLOCK_EXTENT), BLOCK_EXTENT ** -0.5, 0.375, ((0, 32),)),
        "slot_source_sector": place_ends(jax.random.randint(key_of[5], (PAIR_SLOTS_TOTAL,), 0, SECTORS_TOTAL), jax.random.fold_in(key_of[5], 1), 0, SECTORS_TOTAL - 1).astype(jnp.int32),
        "slot_target_sector": place_ends(jax.random.randint(key_of[6], (PAIR_SLOTS_TOTAL,), 0, DEVICE_SECTORS), jax.random.fold_in(key_of[6], 1), 0, DEVICE_SECTORS - 1).astype(jnp.int32),
        "pair_count": draw_pair_count(jax.random.fold_in(key_of[10], 71), 0),
        "left_dims": draw_left_dims(jax.random.fold_in(key_of[10], 71), 0),
        "right_dims": draw_right_dims(jax.random.fold_in(key_of[10], 71), 0),
    }


def block_mask(left_dims, right_dims, block_size):
    positions = jnp.arange(block_size, dtype=jnp.int32)
    return (positions[None, :, None] < left_dims[:, None, None]) & (positions[None, None, :] < right_dims[:, None, None])

def pair_sum(sources, left_operator_blocks, right_operator_blocks, slot_source_sector, target_sector, live_slot):
    zero_sum = jnp.zeros(sources.shape, jnp.float32)

    def add_pair(running, slot_index):

        def compute(running_now):
            source_block = sources[slot_source_sector[slot_index]]
            middle = jnp.dot(left_operator_blocks[slot_index], source_block, preferred_element_type=jnp.float32)
            contribution = jnp.dot(middle, right_operator_blocks[slot_index].astype(jnp.float32), precision=lax.Precision.HIGHEST, preferred_element_type=jnp.float32)
            return running_now.at[target_sector[slot_index]].add(contribution)

        def keep_same(running_now):
            return running_now
        return (lax.cond(live_slot[slot_index], compute, keep_same, running), None)
    slot_ids = jnp.arange(left_operator_blocks.shape[0], dtype=jnp.int32)
    result, _ = lax.scan(add_pair, zero_sum, slot_ids)
    return result

def reference(wavefunction, diagonal, preconditioner, left_operator_blocks, right_operator_blocks, slot_source_sector, slot_target_sector, pair_count, left_dims, right_dims):
    sector_total = wavefunction.shape[0]
    block_size = wavefunction.shape[1]
    entries = float(sector_total * block_size * block_size)
    used_mask = block_mask(left_dims, right_dims, block_size)
    slot_ids = jnp.arange(left_operator_blocks.shape[0], dtype=jnp.int32)
    device_ids = slot_ids // DEVICE_SLOTS
    live_slot = slot_ids % DEVICE_SLOTS < pair_count[device_ids]
    target_sector = (device_ids // N_OP * DEVICE_SECTORS + slot_target_sector).astype(jnp.int32)
    vector = jnp.where(used_mask, wavefunction, jnp.zeros_like(wavefunction))
    vector_float = vector.astype(jnp.float32)
    diag_float = diagonal.astype(jnp.float32)
    sigma_first = jnp.where(used_mask, diag_float * vector_float + pair_sum(vector, left_operator_blocks, right_operator_blocks, slot_source_sector, target_sector, live_slot), 0.0)
    norm_vector = jnp.sum(vector_float * vector_float)
    correlation = jnp.sum(vector_float * sigma_first)
    rayleigh = correlation / norm_vector
    residual = sigma_first - rayleigh * vector_float
    scaled = preconditioner.astype(jnp.float32) * residual
    along_vector = jnp.sum(vector_float * scaled)
    orthogonal = scaled - along_vector / norm_vector * vector_float
    square_norm = jnp.sum(orthogonal * orthogonal)
    correction = (orthogonal * lax.rsqrt(square_norm / entries + 1e-06)).astype(jnp.bfloat16)
    corr_float = correction.astype(jnp.float32)
    product_rows = jnp.where(used_mask, diag_float * corr_float + pair_sum(correction, left_operator_blocks, right_operator_blocks, slot_source_sector, target_sector, live_slot), 0.0)
    cross_term = jnp.sum(vector_float * product_rows)
    self_term = jnp.sum(corr_float * product_rows)
    projected = jnp.stack([rayleigh, cross_term * lax.rsqrt(norm_vector * entries), self_term / entries])
    return (correction, product_rows, projected)
```

```python
import functools

import jax
import jax.numpy as jnp
from jax import lax
from jax.experimental import pallas as pl
from jax.experimental.pallas import tpu as pltpu
from jax.sharding import PartitionSpec as P

MESH = pl.DeviceIdType.MESH
F32 = jnp.float32
BF16 = jnp.bfloat16


def fold_rows(values):
    sums = jnp.sum(values, axis=0, keepdims=True)
    total = sums[:, :128]
    for start in range(128, values.shape[1], 128):
        total = total + sums[:, start : start + 128]
    return total


def make_message(rows):
    blank = jnp.zeros((8 - len(rows), 128), F32)
    return jnp.concatenate(list(rows) + [blank], axis=0)


def davidson_kernel(
    n_sec, n_op, wave, diag, prec, left, right, source, target, count, left_dims, right_dims,
    corr_out, prod_out, proj_out,
    left_v, right_v, all_v, all_c, vec32, diag32, corr32, partial, wire, rs_first, rs_second,
    op_box, sec_box, load_sem, out_sem,
    v_send, v_recv, v_fsend, v_frecv, r1_send, r1_recv, r2_send, r2_recv,
    c_send, c_recv, cy_send, cy_recv, cf_send, cf_recv, op_send, op_recv, sec_send, sec_recv,
):
    sec, op = lax.axis_index("sec"), lax.axis_index("op")
    count_s, block, width = wave.shape
    slots = left.shape[0]
    n_chip = n_sec // 2
    chip, core = sec // 2, lax.rem(sec, 2)
    sibling = sec + 1 - 2 * core
    flat = count_s * block // n_op
    share = block // n_op
    entries = float(n_sec * count_s * block * width)
    first = sec * count_s

    def rotate(index, step, size):
        return lax.rem(index + step + size, size)

    def remote(src, dst, send, recv, device):
        return pltpu.make_async_remote_copy(
            src_ref=src, dst_ref=dst, send_sem=send, recv_sem=recv,
            device_id=device, device_id_type=MESH,
        )

    loads = [
        pltpu.make_async_copy(left, left_v, load_sem.at[0]),
        pltpu.make_async_copy(right, right_v, load_sem.at[1]),
    ]
    for copy in loads:
        copy.start()

    barrier = pltpu.get_barrier_semaphore()
    for step in range(1, n_op):
        pl.semaphore_signal(
            barrier, inc=1, device_id=(sec, rotate(op, step, n_op)), device_id_type=MESH
        )
    for step in range(1, n_sec):
        pl.semaphore_signal(
            barrier, inc=1, device_id=(rotate(sec, step, n_sec), op), device_id_type=MESH
        )

    def used_mask(sector, row_start, rows):
        row = lax.broadcasted_iota(jnp.int32, (rows, width), 0) + row_start
        col = lax.broadcasted_iota(jnp.int32, (rows, width), 1)
        return (row < left_dims[first + sector]) & (col < right_dims[first + sector])

    for t in range(count_s):
        masked = jnp.where(used_mask(t, 0, block), wave[t].astype(F32), 0.0)
        vec32[t] = masked
        all_v[first + t] = masked.astype(BF16)

    pl.semaphore_wait(barrier, n_op - 1 + n_sec - 1)

    sends = []
    for t in range(count_s):
        for step in range(1, n_chip):
            other = rotate(chip, step, n_chip) * 2 + core
            spot = all_v.at[first + t]
            copy = remote(spot, spot, v_send.at[step, t], v_recv.at[step, t], (other, op))
            copy.start()
            sends.append(copy)
    for t in range(count_s):
        spot = all_v.at[first + t]
        copy = remote(spot, spot, v_fsend.at[0, t], v_frecv.at[0, t], (sibling, op))
        copy.start()
        sends.append(copy)
    for t in range(count_s):
        diag32[t] = diag[t].astype(F32)
    for copy in loads:
        copy.wait()
    for t in range(count_s):
        for step in range(1, n_chip):
            origin = rotate(chip, -step, n_chip) * 2 + core
            spot = all_v.at[origin * count_s + t]
            remote(spot, spot, v_send.at[step, t], v_recv.at[step, t], (origin, op)).wait_recv()
            copy = remote(spot, spot, v_fsend.at[step, t], v_frecv.at[step, t], (sibling, op))
            copy.start()
            sends.append(copy)
    for t in range(count_s):
        for step in range(n_chip):
            origin = rotate(chip, -step, n_chip) * 2 + 1 - core
            spot = all_v.at[origin * count_s + t]
            remote(
                spot, spot, v_fsend.at[step, t], v_frecv.at[step, t], (sibling, op)
            ).wait_recv()

    half = block // 2
    group = 4 if slots % 4 == 0 else 1

    def apply_rows(field, row_start):
        for t in range(count_s):
            partial[t, row_start : row_start + half] = jnp.zeros((half, width), F32)

        def some_slots(index, carry):
            sums = [None] * count_s
            for u in range(group):
                k = index * group + u
                live = k < count[0]
                middle = jnp.dot(
                    left_v[k, row_start : row_start + half], field[source[k]],
                    preferred_element_type=F32,
                )
                high = middle.astype(BF16)
                low = (middle - high.astype(F32)).astype(BF16)
                both = jnp.dot(
                    jnp.concatenate([high, low], axis=0), right_v[k],
                    preferred_element_type=F32,
                )
                product = both[:half] + both[half:]
                for t in range(count_s):
                    weight = jnp.where(live & (target[k] == t), 1.0, 0.0).astype(F32)
                    term = product * weight
                    sums[t] = term if sums[t] is None else sums[t] + term
            for t in range(count_s):
                partial[t, row_start : row_start + half] += sums[t]
            return carry

        lax.fori_loop(0, slots // group, some_slots, 0)

    def exchange(turn, rows):
        message = make_message(rows)
        copies = []
        mine = op_box.at[turn, op]
        op_box[turn, op] = message
        for step in range(1, n_op):
            copy = remote(
                mine, mine, op_send.at[turn, step], op_recv.at[turn, step],
                (sec, rotate(op, step, n_op)),
            )
            copy.start()
            copies.append(copy)
        for step in range(1, n_op):
            origin = rotate(op, -step, n_op)
            spot = op_box.at[turn, origin]
            remote(
                spot, spot, op_send.at[turn, step], op_recv.at[turn, step], (sec, origin)
            ).wait_recv()
        total = op_box[turn, 0]
        for index in range(1, n_op):
            total = total + op_box[turn, index]
        mine = sec_box.at[turn, sec]
        sec_box[turn, sec] = total
        for step in range(1, n_sec):
            copy = remote(
                mine, mine, sec_send.at[turn, step], sec_recv.at[turn, step],
                (rotate(sec, step, n_sec), op),
            )
            copy.start()
            copies.append(copy)
        for step in range(1, n_sec):
            origin = rotate(sec, -step, n_sec)
            spot = sec_box.at[turn, origin]
            remote(
                spot, spot, sec_send.at[turn, step], sec_recv.at[turn, step], (origin, op)
            ).wait_recv()
        total = sec_box[turn, 0]
        for index in range(1, n_sec):
            total = total + sec_box[turn, index]
        for copy in copies:
            copy.wait_send()
        return jnp.sum(total, axis=1, keepdims=True)

    def first_copy(dest):
        spot = partial.at[dest * flat // block, pl.ds(dest * flat % block, flat)]
        return remote(spot, rs_first.at[op], r1_send.at[dest], r1_recv.at[op], (sec, dest))

    for part in range(2):
        apply_rows(all_v, part * half)
        for dest in range(n_op):
            if dest * flat % block // half == part:

                @pl.when(dest != op)
                def _():
                    first_copy(dest).start()

    own_sector = op * flat // block
    own_row = pl.multiple_of(lax.rem(op * flat, block), flat)
    own_rows = pl.ds(own_row, flat)
    pairs = partial[own_sector, own_rows]
    for step in range(1, n_op):
        origin = rotate(op, -step, n_op)
        spot = rs_first.at[origin]
        remote(spot, spot, r1_send.at[origin], r1_recv.at[origin], (sec, origin)).wait_recv()
        pairs = pairs + rs_first[origin]

    vector = vec32[own_sector, own_rows]
    scale = prec[own_sector, own_rows].astype(F32)
    sigma = diag32[own_sector, own_rows] * vector + pairs
    sigma = jnp.where(used_mask(own_sector, own_row, flat), sigma, 0.0)
    scaled_vector = scale * vector
    sums = exchange(
        0,
        [
            fold_rows(vector * vector),
            fold_rows(vector * sigma),
            fold_rows(scaled_vector * sigma),
            fold_rows(scaled_vector * vector),
        ],
    )
    norm_vector = sums[0:1]
    rayleigh = sums[1:2] / norm_vector
    along_vector = sums[2:3] - rayleigh * sums[3:4]
    orthogonal = scale * (sigma - rayleigh * vector) - along_vector / norm_vector * vector
    square_norm = exchange(1, [fold_rows(orthogonal * orthogonal)])[0:1]
    correction = orthogonal * lax.rsqrt(square_norm / entries + 1e-06)
    all_c[first + own_sector, own_rows] = correction.astype(BF16)

    def share_of(owner_sec, owner_op):
        row = pl.multiple_of(lax.rem(owner_op * flat, block), flat)
        return all_c.at[owner_sec * count_s + owner_op * flat // block, pl.ds(row, flat)]

    mine = share_of(sec, op)
    for step in range(1, n_op):
        copy = remote(
            mine, mine, c_send.at[step], c_recv.at[step], (sec, rotate(op, step, n_op))
        )
        copy.start()
        sends.append(copy)
    for step in range(n_op):
        origin = rotate(op, -step, n_op)
        spot = share_of(sec, origin)
        if step:
            remote(spot, spot, c_send.at[step], c_recv.at[step], (sec, origin)).wait_recv()
        for jump in range(1, n_chip):
            other = rotate(chip, jump, n_chip) * 2 + core
            copy = remote(
                spot, spot, cy_send.at[jump, step], cy_recv.at[jump, step], (other, op)
            )
            copy.start()
            sends.append(copy)

    def whole_of(owner_sec):
        return all_c.at[pl.ds(owner_sec * count_s, count_s)]

    spot = whole_of(sec)
    copy = remote(spot, spot, cf_send.at[0], cf_recv.at[0], (sibling, op))
    copy.start()
    sends.append(copy)
    out_copy = pltpu.make_async_copy(spot, corr_out, out_sem)
    out_copy.start()
    for t in range(count_s):
        corr32[t] = all_c[first + t].astype(F32)
    for dest in range(n_op):

        @pl.when(dest != op)
        def _():
            first_copy(dest).wait_send()

    for jump in range(1, n_chip):
        owner = rotate(chip, -jump, n_chip) * 2 + core
        for step in range(n_op):
            origin = rotate(op, -step, n_op)
            spot = share_of(owner, origin)
            remote(
                spot, spot, cy_send.at[jump, step], cy_recv.at[jump, step], (owner, op)
            ).wait_recv()
        spot = whole_of(owner)
        copy = remote(spot, spot, cf_send.at[jump], cf_recv.at[jump], (sibling, op))
        copy.start()
        sends.append(copy)
    for jump in range(n_chip):
        owner = rotate(chip, -jump, n_chip) * 2 + 1 - core
        spot = whole_of(owner)
        remote(spot, spot, cf_send.at[jump], cf_recv.at[jump], (sibling, op)).wait_recv()

    narrow = wire is not None
    outgoing = wire if narrow else partial

    def second_copy(dest):
        spot = outgoing.at[:, pl.ds(dest * share, share)]
        return remote(spot, rs_second.at[op], r2_send.at[dest], r2_recv.at[op], (sec, dest))

    for part in range(2):
        apply_rows(all_c, part * half)
        if narrow:
            for t in range(count_s):
                wire[t, part * half : part * half + half] = partial[
                    t, part * half : part * half + half
                ].astype(BF16)
        for dest in range(n_op):
            if dest * share // half == part:

                @pl.when(dest != op)
                def _():
                    second_copy(dest).start()

    share_row = pl.multiple_of(op * share, share)
    share_rows = pl.ds(share_row, share)
    pairs = [partial[t, share_rows] for t in range(count_s)]
    for step in range(1, n_op):
        origin = rotate(op, -step, n_op)
        spot = rs_second.at[origin]
        remote(spot, spot, r2_send.at[origin], r2_recv.at[origin], (sec, origin)).wait_recv()
        for t in range(count_s):
            pairs[t] = pairs[t] + rs_second[origin, t].astype(F32)
    cross, self_sum = None, None
    for t in range(count_s):
        field = corr32[t, share_rows]
        product = diag32[t, share_rows] * field + pairs[t]
        product = jnp.where(used_mask(t, share_row, share), product, 0.0)
        prod_out[t] = product
        cross_part = fold_rows(vec32[t, share_rows] * product)
        self_part = fold_rows(field * product)
        cross = cross_part if t == 0 else cross + cross_part
        self_sum = self_part if t == 0 else self_sum + self_part
    sums = exchange(2, [cross, self_sum])
    proj_out[0] = jnp.sum(rayleigh)
    proj_out[1] = jnp.sum(sums[0:1] * lax.rsqrt(norm_vector * entries))
    proj_out[2] = jnp.sum(sums[1:2] / entries)

    for dest in range(n_op):

        @pl.when(dest != op)
        def _():
            second_copy(dest).wait_send()

    for copy in sends:
        copy.wait_send()
    out_copy.wait()


def on_device(n_sec, n_op, wave, diag, prec, left, right, source, target, count, ldims, rdims):
    count_s, block, width = wave.shape
    slots = left.shape[0]
    sectors = n_sec * count_s
    n_chip = n_sec // 2
    flat = count_s * block // n_op
    share = block // n_op
    narrow = share % 16 == 0
    wire_type = BF16 if narrow else F32
    vmem = pl.BlockSpec(memory_space=pltpu.VMEM)
    smem = pl.BlockSpec(memory_space=pltpu.SMEM)
    hbm = pl.BlockSpec(memory_space=pl.ANY)
    dma = pltpu.SemaphoreType.DMA
    scratch = [
        pltpu.VMEM((slots, block, block), BF16),
        pltpu.VMEM((slots, width, width), BF16),
        pltpu.VMEM((sectors, block, width), BF16),
        pltpu.VMEM((sectors, block, width), BF16),
        pltpu.VMEM((count_s, block, width), F32),
        pltpu.VMEM((count_s, block, width), F32),
        pltpu.VMEM((count_s, block, width), F32),
        pltpu.VMEM((count_s, block, width), F32),
    ]
    if narrow:
        scratch.append(pltpu.VMEM((count_s, block, width), BF16))
    scratch += [
        pltpu.VMEM((n_op, flat, width), F32),
        pltpu.VMEM((n_op, count_s, share, width), wire_type),
        pltpu.VMEM((3, n_op, 8, 128), F32),
        pltpu.VMEM((3, n_sec, 8, 128), F32),
        dma((2,)), dma,
        dma((n_chip, count_s)), dma((n_chip, count_s)),
        dma((n_chip, count_s)), dma((n_chip, count_s)),
        dma((n_op,)), dma((n_op,)), dma((n_op,)), dma((n_op,)),
        dma((n_op,)), dma((n_op,)), dma((n_chip, n_op)), dma((n_chip, n_op)),
        dma((n_chip,)), dma((n_chip,)),
        dma((3, n_op)), dma((3, n_op)), dma((3, n_sec)), dma((3, n_sec)),
    ]

    def body(*refs):
        refs = list(refs)
        if not narrow:
            refs.insert(21, None)
        davidson_kernel(n_sec, n_op, *refs)

    return pl.pallas_call(
        body,
        name="davidson_step",
        out_shape=(
            jax.ShapeDtypeStruct((count_s, block, width), BF16),
            jax.ShapeDtypeStruct((count_s, share, width), F32),
            jax.ShapeDtypeStruct((3,), F32),
        ),
        in_specs=[vmem, vmem, vmem, hbm, hbm, smem, smem, smem, smem, smem],
        out_specs=(hbm, vmem, smem),
        scratch_shapes=scratch,
        compiler_params=pltpu.CompilerParams(
            collective_id=0, has_side_effects=True, vmem_limit_bytes=40 * 1024 * 1024
        ),
        cost_estimate=pl.CostEstimate(
            flops=2 * slots * 6 * block * block * width,
            bytes_accessed=4 * slots * block * block,
            transcendentals=0,
        ),
    )(wave, diag, prec, left, right, source, target, count, ldims, rdims)


def solution(mesh):
    split = P(("sec", "op"))
    in_specs = (
        P("sec", None, None),
        P("sec", None, None),
        P("sec", None, None),
        P(("sec", "op"), None, None),
        P(("sec", "op"), None, None),
        split,
        split,
        split,
        P(),
        P(),
    )
    out_specs = (P("sec", None, None), P("sec", "op", None), P())
    return jax.shard_map(
        functools.partial(on_device, mesh.shape["sec"], mesh.shape["op"]),
        mesh=mesh, in_specs=in_specs, out_specs=out_specs, check_vma=False,
    )
```

```python
import functools

import jax
import jax.numpy as jnp
from jax import lax
from jax.experimental import pallas as pl
from jax.experimental.pallas import tpu as pltpu
from jax.sharding import PartitionSpec as P

MESH = pl.DeviceIdType.MESH
F32 = jnp.float32
BF16 = jnp.bfloat16


def fold_rows(values):
    sums = jnp.sum(values, axis=0, keepdims=True)
    total = sums[:, :128]
    for start in range(128, values.shape[1], 128):
        total = total + sums[:, start : start + 128]
    return total


def make_message(rows):
    blank = jnp.zeros((8 - len(rows), 128), F32)
    return jnp.concatenate(list(rows) + [blank], axis=0)


def davidson_kernel(
    n_sec, n_op, wave_h, diag_h, prec_h, left, right, source_h, target_h, count_h, ldims_h, rdims_h,
    corr_out, prod_out, proj_out,
    left_v, right_v, all_v, all_c, vec32, diag32, corr32, partial, wire, rs_first, rs_second,
    middles, wave, diag, prec, source, target, count, left_dims, right_dims,
    op_box, sec_box, load_sem, out_sem,
    v_send, v_recv, v_fsend, v_frecv, r1_send, r1_recv, r2_send, r2_recv,
    c_send, c_recv, cy_send, cy_recv, cf_send, cf_recv, op_send, op_recv, sec_send, sec_recv,
):
    sec, op = lax.axis_index("sec"), lax.axis_index("op")
    count_s, block, width = wave_h.shape
    slots = left.shape[0]
    n_chip = n_sec // 2
    chip, core = sec // 2, lax.rem(sec, 2)
    sibling = sec + 1 - 2 * core
    flat = count_s * block // n_op
    share = block // n_op
    entries = float(n_sec * count_s * block * width)
    first = sec * count_s

    def rotate(index, step, size):
        return lax.rem(index + step + size, size)

    def remote(src, dst, send, recv, device):
        return pltpu.make_async_remote_copy(
            src_ref=src, dst_ref=dst, send_sem=send, recv_sem=recv,
            device_id=device, device_id_type=MESH,
        )

    pairs_in = [
        (wave_h, wave), (ldims_h, left_dims), (rdims_h, right_dims), (source_h, source),
        (target_h, target), (count_h, count), (diag_h, diag), (prec_h, prec),
        (left, left_v), (right, right_v),
    ]
    loads = [
        pltpu.make_async_copy(src, dst, load_sem.at[index])
        for index, (src, dst) in enumerate(pairs_in)
    ]
    for copy in loads:
        copy.start()

    barrier = pltpu.get_barrier_semaphore()
    for step in range(1, n_op):
        pl.semaphore_signal(
            barrier, inc=1, device_id=(sec, rotate(op, step, n_op)), device_id_type=MESH
        )
    for step in range(1, n_sec):
        pl.semaphore_signal(
            barrier, inc=1, device_id=(rotate(sec, step, n_sec), op), device_id_type=MESH
        )

    for copy in loads[:3]:
        copy.wait()

    def used_mask(sector, row_start, rows):
        row = lax.broadcasted_iota(jnp.int32, (rows, width), 0) + row_start
        col = lax.broadcasted_iota(jnp.int32, (rows, width), 1)
        return (row < left_dims[first + sector]) & (col < right_dims[first + sector])

    for t in range(count_s):
        masked = jnp.where(used_mask(t, 0, block), wave[t].astype(F32), 0.0)
        vec32[t] = masked
        all_v[first + t] = masked.astype(BF16)

    pl.semaphore_wait(barrier, n_op - 1 + n_sec - 1)

    sends = []
    for t in range(count_s):
        for step in range(1, n_chip):
            other = rotate(chip, step, n_chip) * 2 + core
            spot = all_v.at[first + t]
            copy = remote(spot, spot, v_send.at[step, t], v_recv.at[step, t], (other, op))
            copy.start()
            sends.append(copy)
    for t in range(count_s):
        spot = all_v.at[first + t]
        copy = remote(spot, spot, v_fsend.at[0, t], v_frecv.at[0, t], (sibling, op))
        copy.start()
        sends.append(copy)
    for copy in loads[3:]:
        copy.wait()
    for t in range(count_s):
        diag32[t] = diag[t].astype(F32)
    for t in range(count_s):
        for step in range(1, n_chip):
            origin = rotate(chip, -step, n_chip) * 2 + core
            spot = all_v.at[origin * count_s + t]
            remote(spot, spot, v_send.at[step, t], v_recv.at[step, t], (origin, op)).wait_recv()
            copy = remote(spot, spot, v_fsend.at[step, t], v_frecv.at[step, t], (sibling, op))
            copy.start()
            sends.append(copy)
    for t in range(count_s):
        for step in range(n_chip):
            origin = rotate(chip, -step, n_chip) * 2 + 1 - core
            spot = all_v.at[origin * count_s + t]
            remote(
                spot, spot, v_fsend.at[step, t], v_frecv.at[step, t], (sibling, op)
            ).wait_recv()

    half = block // 2
    group = 4 if slots % 4 == 0 else 1

    def fill_middles(field):
        def some_slots(index, carry):
            for u in range(group):
                k = index * group + u
                middle = jnp.dot(left_v[k], field[source[k]], preferred_element_type=F32)
                high = middle.astype(BF16)
                low = (middle - high.astype(F32)).astype(BF16)
                for part in range(2):
                    rows = slice(part * half, part * half + half)
                    middles[k, part, :half] = high[rows]
                    middles[k, part, half:] = low[rows]
            return carry

        lax.fori_loop(0, slots // group, some_slots, 0)

    def apply_rows(part):
        row_start = part * half
        for t in range(count_s):
            partial[t, row_start : row_start + half] = jnp.zeros((half, width), F32)

        def some_slots(index, carry):
            sums = [None] * count_s
            for u in range(group):
                k = index * group + u
                live = k < count[0]
                both = jnp.dot(middles[k, part], right_v[k], preferred_element_type=F32)
                product = both[:half] + both[half:]
                for t in range(count_s):
                    weight = jnp.where(live & (target[k] == t), 1.0, 0.0).astype(F32)
                    term = product * weight
                    sums[t] = term if sums[t] is None else sums[t] + term
            for t in range(count_s):
                partial[t, row_start : row_start + half] += sums[t]
            return carry

        lax.fori_loop(0, slots // group, some_slots, 0)

    def exchange(turn, rows):
        message = make_message(rows)
        copies = []
        mine = op_box.at[turn, op]
        op_box[turn, op] = message
        for step in range(1, n_op):
            copy = remote(
                mine, mine, op_send.at[turn, step], op_recv.at[turn, step],
                (sec, rotate(op, step, n_op)),
            )
            copy.start()
            copies.append(copy)
        for step in range(1, n_op):
            origin = rotate(op, -step, n_op)
            spot = op_box.at[turn, origin]
            remote(
                spot, spot, op_send.at[turn, step], op_recv.at[turn, step], (sec, origin)
            ).wait_recv()
        total = op_box[turn, 0]
        for index in range(1, n_op):
            total = total + op_box[turn, index]
        mine = sec_box.at[turn, sec]
        sec_box[turn, sec] = total
        for step in range(1, n_sec):
            copy = remote(
                mine, mine, sec_send.at[turn, step], sec_recv.at[turn, step],
                (rotate(sec, step, n_sec), op),
            )
            copy.start()
            copies.append(copy)
        for step in range(1, n_sec):
            origin = rotate(sec, -step, n_sec)
            spot = sec_box.at[turn, origin]
            remote(
                spot, spot, sec_send.at[turn, step], sec_recv.at[turn, step], (origin, op)
            ).wait_recv()
        total = sec_box[turn, 0]
        for index in range(1, n_sec):
            total = total + sec_box[turn, index]
        for copy in copies:
            copy.wait_send()
        return jnp.sum(total, axis=1, keepdims=True)

    def first_copy(dest):
        spot = partial.at[dest * flat // block, pl.ds(dest * flat % block, flat)]
        return remote(spot, rs_first.at[op], r1_send.at[dest], r1_recv.at[op], (sec, dest))

    fill_middles(all_v)
    for part in range(2):
        apply_rows(part)
        for dest in range(n_op):
            if dest * flat % block // half == part:

                @pl.when(dest != op)
                def _():
                    first_copy(dest).start()

    own_sector = op * flat // block
    own_row = pl.multiple_of(lax.rem(op * flat, block), flat)
    own_rows = pl.ds(own_row, flat)
    vector = vec32[own_sector, own_rows]
    scale = prec[own_sector, own_rows].astype(F32)
    scaled_vector = scale * vector
    local = diag32[own_sector, own_rows] * vector

    with_vector = fold_rows(vector * local)
    with_scaled = fold_rows(scaled_vector * local)
    for t in range(count_s):
        weighted = vec32[t] * partial[t]
        with_vector = with_vector + fold_rows(weighted)
        with_scaled = with_scaled + fold_rows(weighted * prec[t].astype(F32))
    sums = exchange(
        0,
        [
            fold_rows(vector * vector),
            with_vector,
            with_scaled,
            fold_rows(scaled_vector * vector),
        ],
    )
    norm_vector = sums[0:1]
    rayleigh = sums[1:2] / norm_vector
    along_vector = sums[2:3] - rayleigh * sums[3:4]

    pairs = partial[own_sector, own_rows]
    for step in range(1, n_op):
        origin = rotate(op, -step, n_op)
        spot = rs_first.at[origin]
        remote(spot, spot, r1_send.at[origin], r1_recv.at[origin], (sec, origin)).wait_recv()
        pairs = pairs + rs_first[origin]
    sigma = jnp.where(used_mask(own_sector, own_row, flat), local + pairs, 0.0)
    orthogonal = scale * (sigma - rayleigh * vector) - along_vector / norm_vector * vector
    square_norm = exchange(1, [fold_rows(orthogonal * orthogonal)])[0:1]
    correction = orthogonal * lax.rsqrt(square_norm / entries + 1e-06)
    all_c[first + own_sector, own_rows] = correction.astype(BF16)

    def share_of(owner_sec, owner_op):
        row = pl.multiple_of(lax.rem(owner_op * flat, block), flat)
        return all_c.at[owner_sec * count_s + owner_op * flat // block, pl.ds(row, flat)]

    mine = share_of(sec, op)
    for step in range(1, n_op):
        copy = remote(
            mine, mine, c_send.at[step], c_recv.at[step], (sec, rotate(op, step, n_op))
        )
        copy.start()
        sends.append(copy)
    for step in range(n_op):
        origin = rotate(op, -step, n_op)
        spot = share_of(sec, origin)
        if step:
            remote(spot, spot, c_send.at[step], c_recv.at[step], (sec, origin)).wait_recv()
        for jump in range(1, n_chip):
            other = rotate(chip, jump, n_chip) * 2 + core
            copy = remote(
                spot, spot, cy_send.at[jump, step], cy_recv.at[jump, step], (other, op)
            )
            copy.start()
            sends.append(copy)

    def whole_of(owner_sec):
        return all_c.at[pl.ds(owner_sec * count_s, count_s)]

    spot = whole_of(sec)
    copy = remote(spot, spot, cf_send.at[0], cf_recv.at[0], (sibling, op))
    copy.start()
    sends.append(copy)
    out_copy = pltpu.make_async_copy(spot, corr_out, out_sem)
    out_copy.start()
    for t in range(count_s):
        corr32[t] = all_c[first + t].astype(F32)
    for dest in range(n_op):

        @pl.when(dest != op)
        def _():
            first_copy(dest).wait_send()

    for jump in range(1, n_chip):
        owner = rotate(chip, -jump, n_chip) * 2 + core
        for step in range(n_op):
            origin = rotate(op, -step, n_op)
            spot = share_of(owner, origin)
            remote(
                spot, spot, cy_send.at[jump, step], cy_recv.at[jump, step], (owner, op)
            ).wait_recv()
        spot = whole_of(owner)
        copy = remote(spot, spot, cf_send.at[jump], cf_recv.at[jump], (sibling, op))
        copy.start()
        sends.append(copy)
    for jump in range(n_chip):
        owner = rotate(chip, -jump, n_chip) * 2 + 1 - core
        spot = whole_of(owner)
        remote(spot, spot, cf_send.at[jump], cf_recv.at[jump], (sibling, op)).wait_recv()

    narrow = wire is not None
    outgoing = wire if narrow else partial

    def second_copy(dest):
        spot = outgoing.at[:, pl.ds(dest * share, share)]
        return remote(spot, rs_second.at[op], r2_send.at[dest], r2_recv.at[op], (sec, dest))

    fill_middles(all_c)
    for part in range(2):
        apply_rows(part)
        if narrow:
            for t in range(count_s):
                wire[t, part * half : part * half + half] = partial[
                    t, part * half : part * half + half
                ].astype(BF16)
        for dest in range(n_op):
            if dest * share // half == part:

                @pl.when(dest != op)
                def _():
                    second_copy(dest).start()

    share_row = pl.multiple_of(op * share, share)
    share_rows = pl.ds(share_row, share)
    cross = jnp.zeros((1, 128), F32)
    self_sum = jnp.zeros((1, 128), F32)
    local = []
    for t in range(count_s):
        field = corr32[t, share_rows]
        own = diag32[t, share_rows] * field
        local.append(own)
        cross = cross + fold_rows(vec32[t] * partial[t]) + fold_rows(vec32[t, share_rows] * own)
        self_sum = self_sum + fold_rows(corr32[t] * partial[t]) + fold_rows(field * own)
    sums = exchange(2, [cross, self_sum])
    pairs = [partial[t, share_rows] for t in range(count_s)]
    for step in range(1, n_op):
        origin = rotate(op, -step, n_op)
        spot = rs_second.at[origin]
        remote(spot, spot, r2_send.at[origin], r2_recv.at[origin], (sec, origin)).wait_recv()
        for t in range(count_s):
            pairs[t] = pairs[t] + rs_second[origin, t].astype(F32)
    for t in range(count_s):
        mask = used_mask(t, share_row, share)
        prod_out[t] = jnp.where(mask, local[t] + pairs[t], 0.0)
    proj_out[0] = jnp.sum(rayleigh)
    proj_out[1] = jnp.sum(sums[0:1] * lax.rsqrt(norm_vector * entries))
    proj_out[2] = jnp.sum(sums[1:2] / entries)

    for dest in range(n_op):

        @pl.when(dest != op)
        def _():
            second_copy(dest).wait_send()

    for copy in sends:
        copy.wait_send()
    out_copy.wait()


def on_device(n_sec, n_op, wave, diag, prec, left, right, source, target, count, ldims, rdims):
    count_s, block, width = wave.shape
    slots = left.shape[0]
    sectors = n_sec * count_s
    n_chip = n_sec // 2
    flat = count_s * block // n_op
    share = block // n_op
    narrow = share % 16 == 0
    wire_type = BF16 if narrow else F32
    vmem = pl.BlockSpec(memory_space=pltpu.VMEM)
    smem = pl.BlockSpec(memory_space=pltpu.SMEM)
    hbm = pl.BlockSpec(memory_space=pltpu.HBM)
    dma = pltpu.SemaphoreType.DMA
    scratch = [
        pltpu.VMEM((slots, block, block), BF16),
        pltpu.VMEM((slots, width, width), BF16),
        pltpu.VMEM((sectors, block, width), BF16),
        pltpu.VMEM((sectors, block, width), BF16),
        pltpu.VMEM((count_s, block, width), F32),
        pltpu.VMEM((count_s, block, width), F32),
        pltpu.VMEM((count_s, block, width), F32),
        pltpu.VMEM((count_s, block, width), F32),
    ]
    if narrow:
        scratch.append(pltpu.VMEM((count_s, block, width), BF16))
    scratch += [
        pltpu.VMEM((n_op, flat, width), F32),
        pltpu.VMEM((n_op, count_s, share, width), wire_type),
        pltpu.VMEM((slots, 2, block, width), BF16),
        pltpu.VMEM((count_s, block, width), BF16),
        pltpu.VMEM((count_s, block, width), BF16),
        pltpu.VMEM((count_s, block, width), BF16),
        pltpu.SMEM(source.shape, jnp.int32),
        pltpu.SMEM(target.shape, jnp.int32),
        pltpu.SMEM(count.shape, jnp.int32),
        pltpu.SMEM(ldims.shape, jnp.int32),
        pltpu.SMEM(rdims.shape, jnp.int32),
        pltpu.VMEM((3, n_op, 8, 128), F32),
        pltpu.VMEM((3, n_sec, 8, 128), F32),
        dma((10,)), dma,
        dma((n_chip, count_s)), dma((n_chip, count_s)),
        dma((n_chip, count_s)), dma((n_chip, count_s)),
        dma((n_op,)), dma((n_op,)), dma((n_op,)), dma((n_op,)),
        dma((n_op,)), dma((n_op,)), dma((n_chip, n_op)), dma((n_chip, n_op)),
        dma((n_chip,)), dma((n_chip,)),
        dma((3, n_op)), dma((3, n_op)), dma((3, n_sec)), dma((3, n_sec)),
    ]

    def body(*refs):
        refs = list(refs)
        if not narrow:
            refs.insert(21, None)
        davidson_kernel(n_sec, n_op, *refs)

    return pl.pallas_call(
        body,
        name="davidson_step",
        out_shape=(
            jax.ShapeDtypeStruct((count_s, block, width), BF16),
            jax.ShapeDtypeStruct((count_s, share, width), F32),
            jax.ShapeDtypeStruct((3,), F32),
        ),
        in_specs=[hbm] * 10,
        out_specs=(hbm, vmem, smem),
        scratch_shapes=scratch,
        compiler_params=pltpu.CompilerParams(
            collective_id=0, has_side_effects=True, vmem_limit_bytes=40 * 1024 * 1024
        ),
        cost_estimate=pl.CostEstimate(
            flops=2 * slots * 6 * block * block * width,
            bytes_accessed=4 * slots * block * block,
            transcendentals=0,
        ),
    )(wave, diag, prec, left, right, source, target, count, ldims, rdims)


def solution(mesh):
    split = P(("sec", "op"))
    in_specs = (
        P("sec", None, None),
        P("sec", None, None),
        P("sec", None, None),
        P(("sec", "op"), None, None),
        P(("sec", "op"), None, None),
        split,
        split,
        split,
        P(),
        P(),
    )
    out_specs = (P("sec", None, None), P("sec", "op", None), P())
    return jax.shard_map(
        functools.partial(on_device, mesh.shape["sec"], mesh.shape["op"]),
        mesh=mesh, in_specs=in_specs, out_specs=out_specs, check_vma=False,
    )
```

```python
import functools

import jax
import jax.numpy as jnp
from jax import lax
from jax.experimental import pallas as pl
from jax.experimental.pallas import tpu as pltpu
from jax.sharding import PartitionSpec as P

MESH = pl.DeviceIdType.MESH
F32 = jnp.float32
BF16 = jnp.bfloat16
VMEM_BYTES = 64 * 1024 * 1024
DIRECT_DEVICES = 32


def fold_rows(values):
    sums = jnp.sum(values, axis=0, keepdims=True)
    total = sums[:, :128]
    for start in range(128, values.shape[1], 128):
        total = total + sums[:, start : start + 128]
    return total


def make_message(rows):
    blank = jnp.zeros((8 - len(rows), 128), F32)
    return jnp.concatenate(list(rows) + [blank], axis=0)


def davidson_kernel(
    n_sec, n_op, wave_h, diag_h, prec_h, left, right, source_h, target_h, count_h, ldims_h, rdims_h,
    corr_out, prod_out, proj_out,
    left_v, right_v, all_v, all_c, vec32, diag32, corr32, partial, wire, rs_first, rs_second,
    middles, wave, diag, prec, source, target, count, left_dims, right_dims,
    op_box, sec_box, all_box, all_send, all_recv, load_sem, out_sem,
    v_send, v_recv, v_fsend, v_frecv, r1_send, r1_recv, r2_send, r2_recv,
    c_send, c_recv, cy_send, cy_recv, cf_send, cf_recv, op_send, op_recv, sec_send, sec_recv,
):
    sec, op = lax.axis_index("sec"), lax.axis_index("op")
    count_s, block, width = wave_h.shape
    slots = left.shape[0]
    n_chip = n_sec // 2
    chip, core = sec // 2, lax.rem(sec, 2)
    sibling = sec + 1 - 2 * core
    flat = count_s * block // n_op
    share = block // n_op
    entries = float(n_sec * count_s * block * width)
    first = sec * count_s

    def rotate(index, step, size):
        return lax.rem(index + step + size, size)

    def remote(src, dst, send, recv, device):
        return pltpu.make_async_remote_copy(
            src_ref=src, dst_ref=dst, send_sem=send, recv_sem=recv,
            device_id=device, device_id_type=MESH,
        )

    pairs_in = [
        (wave_h, wave), (ldims_h, left_dims), (rdims_h, right_dims), (source_h, source),
        (target_h, target), (count_h, count), (diag_h, diag), (prec_h, prec),
        (left, left_v), (right, right_v),
    ]
    loads = [
        pltpu.make_async_copy(src, dst, load_sem.at[index])
        for index, (src, dst) in enumerate(pairs_in)
    ]
    for copy in loads:
        copy.start()

    barrier = pltpu.get_barrier_semaphore()
    direct = n_sec * n_op <= DIRECT_DEVICES
    others = [
        (jump, step)
        for jump in range(n_sec)
        for step in range(n_op)
        if jump + step and (direct or jump * step == 0)
    ]

    def other(jump, step):
        return rotate(sec, jump, n_sec), rotate(op, step, n_op)

    for jump, step in others:
        pl.semaphore_signal(barrier, inc=1, device_id=other(jump, step), device_id_type=MESH)

    for copy in loads[:3]:
        copy.wait()

    def used_mask(sector, row_start, rows):
        row = lax.broadcasted_iota(jnp.int32, (rows, width), 0) + row_start
        col = lax.broadcasted_iota(jnp.int32, (rows, width), 1)
        return (row < left_dims[first + sector]) & (col < right_dims[first + sector])

    for t in range(count_s):
        masked = jnp.where(used_mask(t, 0, block), wave[t].astype(F32), 0.0)
        vec32[t] = masked
        all_v[first + t] = masked.astype(BF16)

    pl.semaphore_wait(barrier, len(others))

    sends = []
    for t in range(count_s):
        for step in range(1, n_chip):
            target_sec = rotate(chip, step, n_chip) * 2 + core
            spot = all_v.at[first + t]
            copy = remote(spot, spot, v_send.at[step, t], v_recv.at[step, t], (target_sec, op))
            copy.start()
            sends.append(copy)
    for t in range(count_s):
        spot = all_v.at[first + t]
        copy = remote(spot, spot, v_fsend.at[0, t], v_frecv.at[0, t], (sibling, op))
        copy.start()
        sends.append(copy)
    for copy in loads[3:]:
        copy.wait()
    for t in range(count_s):
        diag32[t] = diag[t].astype(F32)
    for t in range(count_s):
        for step in range(1, n_chip):
            origin = rotate(chip, -step, n_chip) * 2 + core
            spot = all_v.at[origin * count_s + t]
            remote(spot, spot, v_send.at[step, t], v_recv.at[step, t], (origin, op)).wait_recv()
            copy = remote(spot, spot, v_fsend.at[step, t], v_frecv.at[step, t], (sibling, op))
            copy.start()
            sends.append(copy)
    for t in range(count_s):
        for step in range(n_chip):
            origin = rotate(chip, -step, n_chip) * 2 + 1 - core
            spot = all_v.at[origin * count_s + t]
            remote(
                spot, spot, v_fsend.at[step, t], v_frecv.at[step, t], (sibling, op)
            ).wait_recv()

    half = block // 2
    group = 4 if slots % 4 == 0 else 1

    def fill_middles(field):
        def some_slots(index, carry):
            for u in range(group):
                k = index * group + u
                middle = jnp.dot(left_v[k], field[source[k]], preferred_element_type=F32)
                high = middle.astype(BF16)
                low = (middle - high.astype(F32)).astype(BF16)
                for part in range(2):
                    rows = slice(part * half, part * half + half)
                    middles[k, part, :half] = high[rows]
                    middles[k, part, half:] = low[rows]
            return carry

        lax.fori_loop(0, slots // group, some_slots, 0)

    def apply_rows(part):
        row_start = part * half
        for t in range(count_s):
            partial[t, row_start : row_start + half] = jnp.zeros((half, width), F32)

        def some_slots(index, carry):
            sums = [None] * count_s
            for u in range(group):
                k = index * group + u
                live = k < count[0]
                both = jnp.dot(middles[k, part], right_v[k], preferred_element_type=F32)
                product = both[:half] + both[half:]
                for t in range(count_s):
                    weight = jnp.where(live & (target[k] == t), 1.0, 0.0).astype(F32)
                    term = product * weight
                    sums[t] = term if sums[t] is None else sums[t] + term
            for t in range(count_s):
                partial[t, row_start : row_start + half] += sums[t]
            return carry

        lax.fori_loop(0, slots // group, some_slots, 0)

    def exchange(turn, rows):
        message = make_message(rows)
        copies = []
        mine = op_box.at[turn, op]
        op_box[turn, op] = message
        for step in range(1, n_op):
            copy = remote(
                mine, mine, op_send.at[turn, step], op_recv.at[turn, step],
                (sec, rotate(op, step, n_op)),
            )
            copy.start()
            copies.append(copy)
        for step in range(1, n_op):
            origin = rotate(op, -step, n_op)
            spot = op_box.at[turn, origin]
            remote(
                spot, spot, op_send.at[turn, step], op_recv.at[turn, step], (sec, origin)
            ).wait_recv()
        total = op_box[turn, 0]
        for index in range(1, n_op):
            total = total + op_box[turn, index]
        mine = sec_box.at[turn, sec]
        sec_box[turn, sec] = total
        for step in range(1, n_sec):
            copy = remote(
                mine, mine, sec_send.at[turn, step], sec_recv.at[turn, step],
                (rotate(sec, step, n_sec), op),
            )
            copy.start()
            copies.append(copy)
        for step in range(1, n_sec):
            origin = rotate(sec, -step, n_sec)
            spot = sec_box.at[turn, origin]
            remote(
                spot, spot, sec_send.at[turn, step], sec_recv.at[turn, step], (origin, op)
            ).wait_recv()
        total = sec_box[turn, 0]
        for index in range(1, n_sec):
            total = total + sec_box[turn, index]
        for copy in copies:
            copy.wait_send()
        return jnp.sum(total, axis=1, keepdims=True)

    def exchange_direct(rows):
        mine = all_box.at[sec, op]
        all_box[sec, op] = make_message(rows)
        for jump, step in others:
            copy = remote(
                mine, mine, all_send.at[jump, step], all_recv.at[jump, step], other(jump, step)
            )
            copy.start()
            sends.append(copy)
        for jump, step in others:
            origin = other(-jump, -step)
            spot = all_box.at[origin[0], origin[1]]
            remote(
                spot, spot, all_send.at[jump, step], all_recv.at[jump, step], origin
            ).wait_recv()
        parts = [all_box[a, b] for a in range(n_sec) for b in range(n_op)]
        while len(parts) > 1:
            parts = [parts[i] + parts[i + 1] for i in range(0, len(parts), 2)]
        return jnp.sum(parts[0], axis=1, keepdims=True)

    def first_copy(dest):
        spot = partial.at[dest * flat // block, pl.ds(dest * flat % block, flat)]
        return remote(spot, rs_first.at[op], r1_send.at[dest], r1_recv.at[op], (sec, dest))

    fill_middles(all_v)
    for part in range(2):
        apply_rows(part)
        for dest in range(n_op):
            if dest * flat % block // half == part:

                @pl.when(dest != op)
                def _():
                    first_copy(dest).start()

    own_sector = op * flat // block
    own_row = pl.multiple_of(lax.rem(op * flat, block), flat)
    own_rows = pl.ds(own_row, flat)
    vector = vec32[own_sector, own_rows]
    scale = prec[own_sector, own_rows].astype(F32)
    scaled_vector = scale * vector
    local = diag32[own_sector, own_rows] * vector

    with_vector = fold_rows(vector * local)
    with_scaled = fold_rows(scaled_vector * local)
    for t in range(count_s):
        weighted = vec32[t] * partial[t]
        with_vector = with_vector + fold_rows(weighted)
        with_scaled = with_scaled + fold_rows(weighted * prec[t].astype(F32))
    sums = exchange(
        0,
        [
            fold_rows(vector * vector),
            with_vector,
            with_scaled,
            fold_rows(scaled_vector * vector),
        ],
    )
    norm_vector = sums[0:1]
    rayleigh = sums[1:2] / norm_vector
    along_vector = sums[2:3] - rayleigh * sums[3:4]

    pairs = partial[own_sector, own_rows]
    for step in range(1, n_op):
        origin = rotate(op, -step, n_op)
        spot = rs_first.at[origin]
        remote(spot, spot, r1_send.at[origin], r1_recv.at[origin], (sec, origin)).wait_recv()
        pairs = pairs + rs_first[origin]
    sigma = jnp.where(used_mask(own_sector, own_row, flat), local + pairs, 0.0)
    orthogonal = scale * (sigma - rayleigh * vector) - along_vector / norm_vector * vector
    squares = [fold_rows(orthogonal * orthogonal)]
    square_norm = (exchange_direct(squares) if direct else exchange(1, squares))[0:1]
    correction = orthogonal * lax.rsqrt(square_norm / entries + 1e-06)
    all_c[first + own_sector, own_rows] = correction.astype(BF16)

    def share_of(owner_sec, owner_op):
        row = pl.multiple_of(lax.rem(owner_op * flat, block), flat)
        return all_c.at[owner_sec * count_s + owner_op * flat // block, pl.ds(row, flat)]

    mine = share_of(sec, op)
    for step in range(1, n_op):
        copy = remote(
            mine, mine, c_send.at[step], c_recv.at[step], (sec, rotate(op, step, n_op))
        )
        copy.start()
        sends.append(copy)
    for step in range(n_op):
        origin = rotate(op, -step, n_op)
        spot = share_of(sec, origin)
        if step:
            remote(spot, spot, c_send.at[step], c_recv.at[step], (sec, origin)).wait_recv()
        for jump in range(1, n_chip):
            target_sec = rotate(chip, jump, n_chip) * 2 + core
            copy = remote(
                spot, spot, cy_send.at[jump, step], cy_recv.at[jump, step], (target_sec, op)
            )
            copy.start()
            sends.append(copy)

    def whole_of(owner_sec):
        return all_c.at[pl.ds(owner_sec * count_s, count_s)]

    spot = whole_of(sec)
    copy = remote(spot, spot, cf_send.at[0], cf_recv.at[0], (sibling, op))
    copy.start()
    sends.append(copy)
    out_copy = pltpu.make_async_copy(spot, corr_out, out_sem)
    out_copy.start()
    for t in range(count_s):
        corr32[t] = all_c[first + t].astype(F32)
    for dest in range(n_op):

        @pl.when(dest != op)
        def _():
            first_copy(dest).wait_send()

    for jump in range(1, n_chip):
        owner = rotate(chip, -jump, n_chip) * 2 + core
        for step in range(n_op):
            origin = rotate(op, -step, n_op)
            spot = share_of(owner, origin)
            remote(
                spot, spot, cy_send.at[jump, step], cy_recv.at[jump, step], (owner, op)
            ).wait_recv()
        spot = whole_of(owner)
        copy = remote(spot, spot, cf_send.at[jump], cf_recv.at[jump], (sibling, op))
        copy.start()
        sends.append(copy)
    for jump in range(n_chip):
        owner = rotate(chip, -jump, n_chip) * 2 + 1 - core
        spot = whole_of(owner)
        remote(spot, spot, cf_send.at[jump], cf_recv.at[jump], (sibling, op)).wait_recv()

    narrow = wire is not None
    outgoing = wire if narrow else partial

    def second_copy(dest):
        spot = outgoing.at[:, pl.ds(dest * share, share)]
        return remote(spot, rs_second.at[op], r2_send.at[dest], r2_recv.at[op], (sec, dest))

    fill_middles(all_c)
    for part in range(2):
        apply_rows(part)
        if narrow:
            for t in range(count_s):
                wire[t, part * half : part * half + half] = partial[
                    t, part * half : part * half + half
                ].astype(BF16)
        for dest in range(n_op):
            if dest * share // half == part:

                @pl.when(dest != op)
                def _():
                    second_copy(dest).start()

    share_row = pl.multiple_of(op * share, share)
    share_rows = pl.ds(share_row, share)
    cross = jnp.zeros((1, 128), F32)
    self_sum = jnp.zeros((1, 128), F32)
    local = []
    for t in range(count_s):
        field = corr32[t, share_rows]
        own = diag32[t, share_rows] * field
        local.append(own)
        cross = cross + fold_rows(vec32[t] * partial[t]) + fold_rows(vec32[t, share_rows] * own)
        self_sum = self_sum + fold_rows(corr32[t] * partial[t]) + fold_rows(field * own)
    sums = exchange(2, [cross, self_sum])
    pairs = [partial[t, share_rows] for t in range(count_s)]
    for step in range(1, n_op):
        origin = rotate(op, -step, n_op)
        spot = rs_second.at[origin]
        remote(spot, spot, r2_send.at[origin], r2_recv.at[origin], (sec, origin)).wait_recv()
        for t in range(count_s):
            pairs[t] = pairs[t] + rs_second[origin, t].astype(F32)
    for t in range(count_s):
        mask = used_mask(t, share_row, share)
        prod_out[t] = jnp.where(mask, local[t] + pairs[t], 0.0)
    proj_out[0] = jnp.sum(rayleigh)
    proj_out[1] = jnp.sum(sums[0:1] * lax.rsqrt(norm_vector * entries))
    proj_out[2] = jnp.sum(sums[1:2] / entries)

    for dest in range(n_op):

        @pl.when(dest != op)
        def _():
            second_copy(dest).wait_send()

    for copy in sends:
        copy.wait_send()
    out_copy.wait()


def on_device(n_sec, n_op, wave, diag, prec, left, right, source, target, count, ldims, rdims):
    count_s, block, width = wave.shape
    slots = left.shape[0]
    sectors = n_sec * count_s
    n_chip = n_sec // 2
    flat = count_s * block // n_op
    share = block // n_op
    narrow = share % 16 == 0
    wire_type = BF16 if narrow else F32
    vmem = pl.BlockSpec(memory_space=pltpu.VMEM)
    smem = pl.BlockSpec(memory_space=pltpu.SMEM)
    hbm = pl.BlockSpec(memory_space=pltpu.HBM)
    dma = pltpu.SemaphoreType.DMA
    scratch = [
        pltpu.VMEM((slots, block, block), BF16),
        pltpu.VMEM((slots, width, width), BF16),
        pltpu.VMEM((sectors, block, width), BF16),
        pltpu.VMEM((sectors, block, width), BF16),
        pltpu.VMEM((count_s, block, width), F32),
        pltpu.VMEM((count_s, block, width), F32),
        pltpu.VMEM((count_s, block, width), F32),
        pltpu.VMEM((count_s, block, width), F32),
    ]
    if narrow:
        scratch.append(pltpu.VMEM((count_s, block, width), BF16))
    scratch += [
        pltpu.VMEM((n_op, flat, width), F32),
        pltpu.VMEM((n_op, count_s, share, width), wire_type),
        pltpu.VMEM((slots, 2, block, width), BF16),
        pltpu.VMEM((count_s, block, width), BF16),
        pltpu.VMEM((count_s, block, width), BF16),
        pltpu.VMEM((count_s, block, width), BF16),
        pltpu.SMEM(source.shape, jnp.int32),
        pltpu.SMEM(target.shape, jnp.int32),
        pltpu.SMEM(count.shape, jnp.int32),
        pltpu.SMEM(ldims.shape, jnp.int32),
        pltpu.SMEM(rdims.shape, jnp.int32),
        pltpu.VMEM((3, n_op, 8, 128), F32),
        pltpu.VMEM((3, n_sec, 8, 128), F32),
        pltpu.VMEM((n_sec, n_op, 8, 128), F32), dma((n_sec, n_op)), dma((n_sec, n_op)),
        dma((10,)), dma,
        dma((n_chip, count_s)), dma((n_chip, count_s)),
        dma((n_chip, count_s)), dma((n_chip, count_s)),
        dma((n_op,)), dma((n_op,)), dma((n_op,)), dma((n_op,)),
        dma((n_op,)), dma((n_op,)), dma((n_chip, n_op)), dma((n_chip, n_op)),
        dma((n_chip,)), dma((n_chip,)),
        dma((3, n_op)), dma((3, n_op)), dma((3, n_sec)), dma((3, n_sec)),
    ]

    def body(*refs):
        refs = list(refs)
        if not narrow:
            refs.insert(21, None)
        davidson_kernel(n_sec, n_op, *refs)

    return pl.pallas_call(
        body,
        name="davidson_step",
        out_shape=(
            jax.ShapeDtypeStruct((count_s, block, width), BF16),
            jax.ShapeDtypeStruct((count_s, share, width), F32),
            jax.ShapeDtypeStruct((3,), F32),
        ),
        in_specs=[hbm] * 10,
        out_specs=(hbm, vmem, smem),
        scratch_shapes=scratch,
        compiler_params=pltpu.CompilerParams(
            collective_id=0, has_side_effects=True, vmem_limit_bytes=VMEM_BYTES
        ),
        cost_estimate=pl.CostEstimate(
            flops=2 * slots * 6 * block * block * width,
            bytes_accessed=4 * slots * block * block,
            transcendentals=0,
        ),
    )(wave, diag, prec, left, right, source, target, count, ldims, rdims)


def solution(mesh):
    split = P(("sec", "op"))
    in_specs = (
        P("sec", None, None),
        P("sec", None, None),
        P("sec", None, None),
        P(("sec", "op"), None, None),
        P(("sec", "op"), None, None),
        split,
        split,
        split,
        P(),
        P(),
    )
    out_specs = (P("sec", None, None), P("sec", "op", None), P())
    return jax.shard_map(
        functools.partial(on_device, mesh.shape["sec"], mesh.shape["op"]),
        mesh=mesh, in_specs=in_specs, out_specs=out_specs, check_vma=False,
    )
```
